32 devices in a mesh: dp: 2 (over x), pipe: 4 (over z), tensor: 4 (over y, core).
Axes of the slice: x: 2, y: 2, z: 4, core: 2. Of those that a mesh axis runs over, the one named last changes fastest.
Arguments:
- upstream: bfloat16 [4, 2, 1024, 6144], P('pipe', 'dp', 'tensor')
- inputs: bfloat16 [4, 2, 1024, 6144], P('pipe', 'dp', 'tensor')
- keys: bfloat16 [4, 2, 1024, 6144], P('pipe', 'dp', None, 'tensor')
- values: bfloat16 [4, 2, 1024, 6144], P('pipe', 'dp', None, 'tensor'), may hold values from -6 to 6
- gain: float32 [4, 6144], P('pipe'), may hold values from 0.5 to 1.5
Outputs:
- grad_inputs: bfloat16 [4, 2, 1024, 6144], P('pipe', 'dp', 'tensor')
- grad_keys: bfloat16 [4, 2, 1024, 6144], P('pipe', 'dp', None, 'tensor')
- grad_values: bfloat16 [4, 2, 1024, 6144], P('pipe', 'dp', None, 'tensor')
- grad_gain: float32 [4, 6144], P('pipe', 'tensor')
The draws below stay inside these ranges and needn't reach their ends.
All inputs are finite; a program needn't handle non-finite values.
Results may differ from the reference program's by a relative error of at most 0.02.
The reference program's roundings to bfloat16 on the way (of `incoming`, `normed_b`, `queries`, `weights_narrow`, `grad_scores` and `grad_queries`) count: a program that leaves them out, or rounds other values in their place, can miss the bound.
Values may be sent and summed in bfloat16 or wider, within the bound.
No kernel may reach another device: no remote copies, remote signals or barrier semaphores. Data moves between devices by JAX's collectives and lax.ppermute only.
A program may use at most 192 MiB of HBM per device.

```python
import math
import jax
import jax.numpy as jnp
from jax import lax

HEADS = 48
HEAD_DIM = 128
D = 6144
SEQ = 1024
SECTIONS = 4
MICRO = 2


def base_rows(key):
    return jax.random.normal(jax.random.fold_in(key, 101), (SECTIONS, MICRO, SEQ, D), jnp.float32)


def draw_inputs(key, part):
    own_key = jax.random.fold_in(key, 1)
    samples = base_rows(key)
    logs = jax.random.uniform(own_key, (SECTIONS, MICRO, SEQ, 1), jnp.float32, math.log(0.3), math.log(3.0))
    return (samples * jnp.exp(logs)).astype(jnp.bfloat16)


def draw_keys(key, part):
    own_key = jax.random.fold_in(key, 2)
    drawn = 1.5 * jax.random.normal(jax.random.fold_in(own_key, 0), (SECTIONS, MICRO, SEQ, D), jnp.float32)
    return drawn.astype(jnp.bfloat16)


def draw_upstream(key, part):
    own_key = jax.random.fold_in(key, 3)
    samples = jax.random.normal(jax.random.fold_in(own_key, 0), (SECTIONS, MICRO, SEQ, D), jnp.float32)
    position_share = (jnp.arange(MICRO)[:, None] * SEQ + jnp.arange(SEQ)[None, :]).astype(jnp.float32) / (MICRO * SEQ - 1)
    rising = jnp.exp(math.log(3.0) * position_share)[None, :, :, None]
    return (samples * rising).astype(jnp.bfloat16)


def steps_of(key, dims, cuts, smallest, largest):
    def one(axis_at, shards_of):
        draws = jax.random.uniform(jax.random.fold_in(jax.random.fold_in(key, 6), axis_at), (shards_of,), jnp.float32, smallest / len(cuts), largest / len(cuts))
        return jnp.repeat(jnp.exp(draws), dims[axis_at] // shards_of).reshape((-1,) + (1,) * (len(dims) - axis_at - 1))

    factor_of = one(*cuts[0])
    for cut in cuts[1:]:
        factor_of = factor_of * one(*cut)
    return factor_of


def gaussian(rng, extent, scale, reach, split=(), held_as=jnp.bfloat16):
    loudness = steps_of(rng, extent, split, -0.22, 0.18) if split else 1.0
    values = jax.random.normal(rng, extent, jnp.float32) * scale * loudness
    return jnp.minimum(jnp.maximum(values, -reach), reach).astype(held_as)


def setup_inputs(seed: int = 0) -> dict:
    streams_of = jax.random.split(jax.random.key(seed), 6)
    upstream = draw_upstream(jax.random.fold_in(streams_of[5], 71), 0)
    inputs = draw_inputs(jax.random.fold_in(streams_of[5], 71), 0)
    keys = draw_keys(jax.random.fold_in(streams_of[5], 71), 0)
    values = gaussian(streams_of[3], (SECTIONS, MICRO, SEQ, D), 1.0, 6.0, ((0, 4), (1, 2), (3, 4)))
    gain = jnp.clip(1.0 + 0.1 * jax.random.normal(streams_of[4], (SECTIONS, D), jnp.float32), 0.5, 1.5)
    return {"upstream": upstream, "inputs": inputs, "keys": keys, "values": values, "gain": gain}


EPSILON = 1e-05

def narrow(value):
    return lax.optimization_barrier(value.astype(jnp.bfloat16))

def micro_backward(incoming, inputs, keys, values, gain):
    head_shape = (SEQ, HEADS, HEAD_DIM)
    inputs_wide = inputs.astype(jnp.float32)
    root_mean = jnp.sqrt(lax.optimization_barrier(jnp.mean(inputs_wide * inputs_wide, axis=-1, keepdims=True)) + EPSILON)
    normed = inputs_wide / root_mean
    normed_b = narrow(normed).astype(jnp.float32)
    queries = narrow(normed_b * gain).astype(jnp.float32)
    query_heads = queries.reshape(head_shape)
    key_heads = keys.astype(jnp.float32).reshape(head_shape)
    value_heads = values.astype(jnp.float32).reshape(head_shape)
    grad_out = incoming.astype(jnp.float32).reshape(head_shape)
    scaling = 1.0 / math.sqrt(HEAD_DIM)
    scores = jnp.einsum('qhd,khd->hqk', query_heads, key_heads) * scaling
    causal = jnp.arange(SEQ)[:, None] >= jnp.arange(SEQ)[None, :]
    scores = jnp.where(causal[None], scores, -jnp.inf)
    row_max = lax.optimization_barrier(jnp.max(scores, axis=-1, keepdims=True))
    log_total = row_max + jnp.log(lax.optimization_barrier(jnp.sum(jnp.exp(scores - row_max), axis=-1, keepdims=True)))
    softmax_weights = jnp.exp(scores - log_total)
    weights_narrow = narrow(softmax_weights).astype(jnp.float32)
    grad_weights = jnp.einsum('qhd,khd->hqk', grad_out, value_heads)
    row_delta = lax.optimization_barrier(jnp.sum(softmax_weights * grad_weights, axis=-1, keepdims=True))
    grad_scores = narrow(softmax_weights * (grad_weights - row_delta) * scaling).astype(jnp.float32)
    grad_values = jnp.einsum('hqk,qhd->khd', weights_narrow, grad_out).reshape(SEQ, D)
    grad_keys = jnp.einsum('hqk,qhd->khd', grad_scores, query_heads).reshape(SEQ, D)
    grad_queries = narrow(jnp.einsum('hqk,khd->qhd', grad_scores, key_heads).reshape(SEQ, D)).astype(jnp.float32)
    partial_gain = lax.optimization_barrier(jnp.sum(grad_queries * normed_b, axis=0))
    scaled = grad_queries * gain
    grad_inputs = incoming.astype(jnp.float32) + (scaled - normed * lax.optimization_barrier(jnp.mean(scaled * normed, axis=-1, keepdims=True))) / root_mean
    return (grad_inputs.astype(jnp.bfloat16), grad_keys.astype(jnp.bfloat16), grad_values.astype(jnp.bfloat16), partial_gain)

def section_backward(packed):
    incoming, inputs, keys, values, gain = packed

    def one_micro(pieces):
        return micro_backward(pieces[0], pieces[1], pieces[2], pieces[3], gain)
    results = lax.map(one_micro, (incoming, inputs, keys, values))
    return (results[0], results[1], results[2], lax.optimization_barrier(jnp.sum(results[3], axis=0)))

def reference(upstream, inputs, keys, values, gain):
    incoming = jnp.roll(upstream, -1, axis=0)
    grad_inputs, grad_keys, grad_values, grad_gain = lax.map(section_backward, (incoming, inputs, keys, values, gain))
    return (grad_inputs, grad_keys, grad_values, grad_gain)
```

```python
import functools
import math

import jax
import jax.numpy as jnp
from jax import lax
from jax.experimental import pallas as pl
from jax.experimental.pallas import tpu as pltpu
from jax.sharding import PartitionSpec as P

HEAD_DIM = 128
EPSILON = 1e-05
CHUNKS = 3
BLOCK = 256
HEADS_A_STEP = 2
MIB = 1 << 20


def params(limit):
    return pltpu.CompilerParams(vmem_limit_bytes=limit * MIB)


def cost(flops, moved, exps=0):
    return pl.CostEstimate(flops=flops, bytes_accessed=moved, transcendentals=exps)


def made(shape, dtype=jnp.bfloat16):
    return jax.ShapeDtypeStruct(shape, dtype)


def cut(columns, chunks):
    heads = columns // HEAD_DIM
    chunks = min(chunks, heads)
    bounds = [-(-heads * c // chunks) * HEAD_DIM for c in range(chunks + 1)]
    return [(start, end - start) for start, end in zip(bounds, bounds[1:])]


def pinned(x):
    return pltpu.with_memory_space_constraint(x, pltpu.HBM)


def prepare_kernel(shares, ranks, steps, rank_ref, upstream_ref, inputs_ref, *refs):
    *out_refs, upstream_held, inputs_held, arrived = refs
    handed_refs, normed_refs = out_refs[: len(shares)], out_refs[len(shares) :]
    block_rows = inputs_ref.shape[0] // steps
    columns = inputs_ref.shape[1] // ranks
    step = pl.program_id(0)

    def copies(i):
        down = pl.ds(pl.multiple_of(i * block_rows, block_rows), block_rows)
        return [
            pltpu.make_async_copy(source.at[down, :], held.at[down, :], arrived.at[n, i])
            for n, (source, held) in enumerate(((inputs_ref, inputs_held), (upstream_ref, upstream_held)))
        ]

    @pl.when(step == 0)
    def _():
        for i in range(steps):
            for copy in copies(i):
                copy.start()

    for copy in copies(step):
        copy.wait()
    down = pl.ds(pl.multiple_of(step * block_rows, block_rows), block_rows)
    x = inputs_held[down, :].astype(jnp.float32)
    inverse = 1.0 / jnp.sqrt(jnp.mean(x * x, axis=-1, keepdims=True) + EPSILON)
    for c, (start, wide) in enumerate(shares):
        for k in range(ranks):
            at = pl.ds(pl.multiple_of((rank_ref[0] ^ k) * columns + start, HEAD_DIM), wide)
            handed_refs[c][k] = upstream_held[down, at]
            piece = inputs_held[down, at].astype(jnp.float32)
            normed_refs[c * ranks + k][...] = (piece * inverse).astype(jnp.bfloat16)


def prepare(rank, upstream, inputs, shares, ranks, block_rows):
    length, features = inputs.shape
    steps = length // block_rows
    whole = pl.BlockSpec(memory_space=pl.ANY)
    outs = pl.pallas_call(
        functools.partial(prepare_kernel, shares, ranks, steps),
        grid_spec=pltpu.PrefetchScalarGridSpec(
            num_scalar_prefetch=1,
            grid=(steps,),
            in_specs=[whole, whole],
            out_specs=[pl.BlockSpec((ranks, block_rows, wide), lambda i, _: (0, i, 0)) for _, wide in shares]
            + [pl.BlockSpec((block_rows, wide), lambda i, _: (i, 0)) for _, wide in shares for _ in range(ranks)],
            scratch_shapes=[pltpu.VMEM((length, features), jnp.bfloat16)] * 2
            + [pltpu.SemaphoreType.DMA((2, steps))],
        ),
        out_shape=[made((ranks, length, wide)) for _, wide in shares]
        + [
            made((length, wide)) if k else pltpu.HBM((length, wide), jnp.bfloat16)
            for _, wide in shares
            for k in range(ranks)
        ],
        compiler_params=params(14),
        cost_estimate=cost(4 * inputs.size, 8 * inputs.size),
    )(rank, pinned(upstream), pinned(inputs))
    normed = outs[len(shares) :]
    return outs[: len(shares)], [normed[c * ranks : (c + 1) * ranks] for c in range(len(shares))]


def folded(x):
    return jnp.sum(x.reshape(x.shape[0] // 8, 8, x.shape[1]), axis=0)


def attention_kernel(ranks, rank_ref, *refs):
    normed_refs, grad_out_refs = refs[:ranks], refs[ranks : 2 * ranks]
    keys_ref, values_ref, gain_ref = refs[2 * ranks : 2 * ranks + 3]
    *grad_queries_refs, grad_keys_ref, grad_values_ref, grad_gain_ref, normed_ref, out_ref, turned_ref = refs[
        -ranks - 6 :
    ]
    tokens = grad_queries_refs[0].shape[0]
    length, wide = keys_ref.shape
    block = min(BLOCK, length)
    blocks = length // block
    scaling = 1.0 / math.sqrt(HEAD_DIM)
    base = scaling * math.log2(math.e)

    def rows_of(k):
        return pl.ds(pl.multiple_of((rank_ref[0] ^ k) * tokens, tokens), tokens)

    for k in range(ranks):
        normed_ref[rows_of(k), :] = normed_refs[k][...]
        out_ref[rows_of(k), :] = grad_out_refs[k][0] if k == 0 else grad_out_refs[k][...]

    key_at = lax.broadcasted_iota(jnp.int32, (block, block), 0)
    query_at = lax.broadcasted_iota(jnp.int32, (block, block), 1)
    allowed = key_at <= query_at
    across = (((1,), (1,)), ((), ()))

    def rows(x, i):
        return x[i * block : (i + 1) * block]

    heads = []
    for start in range(0, wide, HEAD_DIM):
        at = slice(start, start + HEAD_DIM)
        keys = keys_ref[:, at]
        heads.append(
            dict(
                at=at,
                queries=(normed_ref[:, at].astype(jnp.float32) * gain_ref[:, at]).astype(jnp.bfloat16),
                grad_out=out_ref[:, at],
                keys=keys,
                values=values_ref[:, at],
                keys_turned=keys.T,
                grad_keys=[None] * blocks,
                grad_values=[None] * blocks,
            )
        )

    def product(head, i, j):
        score = lax.dot_general(
            rows(head["keys"], j), rows(head["queries"], i), across, preferred_element_type=jnp.float32
        )
        weighed = lax.dot_general(
            rows(head["values"], j), rows(head["grad_out"], i), across, preferred_element_type=jnp.float32
        )
        score = jnp.where(allowed, score, -jnp.inf) if j == i else score
        return score, weighed, jnp.max(score.reshape(block // 8, 8, block), axis=0)

    def joined(x, y):
        return y if x is None else x + y

    stages = [(head, i) for head in heads for i in range(blocks)]
    ready = [product(*stages[0], j) for j in range(stages[0][1] + 1)]
    for at, (head, i) in enumerate(stages):
        tiles, ready = ready, []
        later = [(*stages[at + 1], j) for j in range(stages[at + 1][1] + 1)] if at + 1 < len(stages) else []
        top = functools.reduce(jnp.maximum, [t[2] for t in tiles])
        shift = jnp.max(top, axis=0, keepdims=True) * base
        exps, total, slope = [], None, None
        for j, (score, weighed, _) in enumerate(tiles):
            e = jnp.exp2(score * base - shift)
            exps.append(e)
            total = joined(total, folded(e))
            slope = joined(slope, folded(e * weighed))
            if later:
                ready.append(product(*later.pop(0)))
        ready += [product(*one) for one in later]
        inverse = 1.0 / jnp.sum(total, axis=0, keepdims=True)
        delta = jnp.sum(slope, axis=0, keepdims=True) * inverse
        query, grad = rows(head["queries"], i), rows(head["grad_out"], i)
        turned = None
        for j, (_, weighed, _) in enumerate(tiles):
            weights = exps[j] * inverse
            narrow = weights.astype(jnp.bfloat16)
            slopes = (weights * (weighed - delta) * scaling).astype(jnp.bfloat16)
            head["grad_values"][j] = joined(
                head["grad_values"][j], jnp.dot(narrow, grad, preferred_element_type=jnp.float32)
            )
            head["grad_keys"][j] = joined(
                head["grad_keys"][j], jnp.dot(slopes, query, preferred_element_type=jnp.float32)
            )
            keys_turned = head["keys_turned"][:, j * block : (j + 1) * block]
            turned = joined(turned, jnp.dot(keys_turned, slopes, preferred_element_type=jnp.float32))
        turned_ref[i * block : (i + 1) * block, head["at"]] = turned.T.astype(jnp.bfloat16)
        if i == blocks - 1:
            for j in range(blocks):
                down = slice(j * block, (j + 1) * block)
                grad_keys_ref[down, head["at"]] = head["grad_keys"][j].astype(jnp.bfloat16)
                grad_values_ref[down, head["at"]] = head["grad_values"][j].astype(jnp.bfloat16)

    grad_gain_ref[...] = jnp.sum(
        folded(turned_ref[...].astype(jnp.float32) * normed_ref[...].astype(jnp.float32)), axis=0, keepdims=True
    )
    for k, grad_queries_ref in enumerate(grad_queries_refs):
        grad_queries_ref[...] = turned_ref[rows_of(k), :]


def attention_back(share, rank, normed, grad_out, keys, values, gain, earlier):
    start, wide = share
    heads = wide // HEAD_DIM
    step = math.gcd(math.gcd(start, wide), HEADS_A_STEP * HEAD_DIM)
    first = start // step
    ranks, tokens = len(normed), normed[0].shape[0]
    length = keys.shape[0]
    own = pl.BlockSpec((tokens, step), lambda h, _: (0, h))
    first_piece = pl.BlockSpec((1, tokens, step), lambda h, _: (0, 0, h))
    placed = pl.BlockSpec((length, step), lambda h, _: (0, first + h))
    pairs = length * length * heads
    outs = pl.pallas_call(
        functools.partial(attention_kernel, ranks),
        grid_spec=pltpu.PrefetchScalarGridSpec(
            num_scalar_prefetch=1,
            grid=(wide // step,),
            in_specs=[own] * ranks
            + [first_piece]
            + [own] * (ranks - 1)
            + [placed, placed, pl.BlockSpec((1, step), lambda h, _: (0, first + h))]
            + [pl.BlockSpec(memory_space=pl.ANY)] * len(earlier),
            out_specs=[own] * ranks
            + [placed, placed, pl.BlockSpec((1, step), lambda h, _: (0, h))],
            scratch_shapes=[pltpu.VMEM((length, step), jnp.bfloat16)] * 3,
        ),
        out_shape=[made((tokens, wide))] * ranks
        + [pltpu.HBM(keys.shape, jnp.bfloat16)] * 2
        + [made((1, wide), jnp.float32)],
        input_output_aliases={2 * ranks + 4 + i: ranks + i for i in range(len(earlier))},
        compiler_params=params(20),
        cost_estimate=cost(10 * pairs * HEAD_DIM, 8 * pairs, pairs),
    )(rank, *normed, *grad_out, pinned(keys), pinned(values), gain, *earlier)
    return outs[:ranks], outs[ranks : ranks + 2], outs[-1]


def finish_kernel(shares, ranks, rank_ref, inputs_ref, gain_ref, *refs):
    incoming_refs, grad_refs, out_ref = refs[: len(shares)], refs[len(shares) : -1], refs[-1]
    features = inputs_ref.shape[1]
    columns = features // ranks

    def pieces():
        for c, (start, wide) in enumerate(shares):
            for k in range(ranks):
                at = pl.ds(pl.multiple_of((rank_ref[0] ^ k) * columns + start, HEAD_DIM), wide)
                x = inputs_ref[:, at].astype(jnp.float32)
                scaled = grad_refs[c * ranks + k][...].astype(jnp.float32) * gain_ref[:, at]
                yield c, k, at, x, scaled

    def along(terms):
        return jnp.sum(sum(terms), axis=-1, keepdims=True)

    def lanes(x):
        return sum(x[:, i : i + HEAD_DIM] for i in range(0, x.shape[1], HEAD_DIM))

    squares, products = [], []
    for _, _, _, x, scaled in pieces():
        squares.append(lanes(x * x))
        products.append(lanes(scaled * x))
    inverse = 1.0 / jnp.sqrt(along(squares) / features + EPSILON)
    slope = along(products) / features * inverse * inverse * inverse
    for c, k, at, x, scaled in pieces():
        incoming = incoming_refs[c][k].astype(jnp.float32)
        out_ref[:, at] = (incoming + (scaled * inverse - x * slope)).astype(jnp.bfloat16)


def finish(rank, inputs, gain, incoming, grads, shares, block_rows):
    length, features = inputs.shape
    ranks = len(grads[0])
    flat = pl.BlockSpec((block_rows, features), lambda i, _: (i, 0))
    return pl.pallas_call(
        functools.partial(finish_kernel, shares, ranks),
        grid_spec=pltpu.PrefetchScalarGridSpec(
            num_scalar_prefetch=1,
            grid=(length // block_rows,),
            in_specs=[flat, pl.BlockSpec((1, features), lambda i, _: (0, 0))]
            + [pl.BlockSpec((ranks, block_rows, wide), lambda i, _: (0, i, 0)) for _, wide in shares]
            + [pl.BlockSpec((block_rows, wide), lambda i, _: (i, 0)) for _, wide in shares for _ in range(ranks)],
            out_specs=flat,
        ),
        out_shape=made(inputs.shape),
        compiler_params=params(16),
        cost_estimate=cost(12 * inputs.size, 8 * inputs.size),
    )(rank, inputs, gain, *incoming, *[x for part in grads for x in part])


def from_behind(x, axis, by):
    devices = lax.axis_size(axis)
    return lax.ppermute(x, axis, [(i, (i + by) % devices) for i in range(devices)])


def total(x, axis):
    passing, result = x, x
    for _ in range(lax.axis_size(axis) - 1):
        passing = from_behind(passing, axis, 1)
        result = result + passing
    return result


def after(values, events):
    return lax.optimization_barrier((tuple(values), tuple(events)))[0]


def swapped(pieces, earlier=None):
    devices = lax.axis_size("tensor")
    results = [pieces[0]]
    for k in range(1, devices):
        piece = after(pieces[k : k + 1], earlier[k : k + 1])[0] if earlier else pieces[k]
        results.append(lax.ppermute(piece, "tensor", [(i, i ^ k) for i in range(devices)]))
    return results


def body(upstream, inputs, keys, values, gain):
    ranks = lax.axis_size("tensor")
    tokens = inputs.shape[2]
    columns = keys.shape[3]
    shares = cut(columns, CHUNKS)

    upstream, inputs = upstream[0, 0], inputs[0, 0]
    keys, values = keys[0, 0], values[0, 0]
    rank = lax.axis_index("tensor")
    gain_columns = lax.dynamic_slice_in_dim(gain, rank * columns, columns, 1)
    rank = rank[None]

    handed, normed = prepare(rank, upstream, inputs, shares, ranks, min(64, tokens))

    latest = None
    for c, pieces in enumerate(normed):
        normed[c] = latest = swapped(pieces, latest)
    incoming = []
    for c, held in enumerate(handed):
        if c >= 2:
            (held,) = after([held], [incoming[c - 2]])
        incoming.append(from_behind(held, "pipe", -1))
    grad_out = []
    for held in incoming:
        latest = swapped([held] + [held[k] for k in range(1, ranks)], latest)
        grad_out.append(latest)

    grads, gain_parts, earlier = [], [], ()
    for c, share in enumerate(shares):
        if 0 < c < len(shares) - 1:
            grad_out[c] = list(after(grad_out[c], [incoming[c + 1]]))
        grad_queries, earlier, gain_part = attention_back(
            share, rank, normed[c], grad_out[c], keys, values, gain_columns, earlier
        )
        gain_parts.append(gain_part)
        grads.append(swapped(grad_queries, grads[-1] if grads else None))
    grad_keys, grad_values = earlier
    grad_gain = total(jnp.concatenate(gain_parts, axis=1), "dp")
    grad_inputs = finish(rank, inputs, gain, incoming, grads, shares, min(64, tokens))
    return (
        grad_inputs[None, None],
        grad_keys[None, None],
        grad_values[None, None],
        grad_gain,
    )


def solution(mesh):
    in_specs = (
        P("pipe", "dp", "tensor", None),
        P("pipe", "dp", "tensor", None),
        P("pipe", "dp", None, "tensor"),
        P("pipe", "dp", None, "tensor"),
        P("pipe", None),
    )
    out_specs = (
        P("pipe", "dp", "tensor", None),
        P("pipe", "dp", None, "tensor"),
        P("pipe", "dp", None, "tensor"),
        P("pipe", "tensor"),
    )
    return jax.shard_map(body, mesh=mesh, in_specs=in_specs, out_specs=out_specs, check_vma=False)
```

```python
import functools
import math

import jax
import jax.numpy as jnp
from jax import lax
from jax.experimental import pallas as pl
from jax.experimental.pallas import tpu as pltpu
from jax.sharding import PartitionSpec as P

HEAD_DIM = 128
EPSILON = 1e-05
PARTS = (4, 9, 12)
BLOCK = 256
HEADS_A_STEP = 1
MIB = 1 << 20


def params(limit):
    return pltpu.CompilerParams(vmem_limit_bytes=limit * MIB)


def cost(flops, moved, exps=0):
    return pl.CostEstimate(flops=flops, bytes_accessed=moved, transcendentals=exps)


def made(shape, dtype=jnp.bfloat16):
    return jax.ShapeDtypeStruct(shape, dtype)


def cut(columns):
    heads = columns // HEAD_DIM
    bounds = [0] + [heads * part // PARTS[-1] * HEAD_DIM for part in PARTS]
    return [(start, end - start) for start, end in zip(bounds, bounds[1:]) if end > start]


def pinned(x):
    return pltpu.with_memory_space_constraint(x, pltpu.HBM)


def lead_kernel(share, ranks, rank_ref, upstream_ref, out_ref, arrived):
    start, wide = share
    columns = upstream_ref.shape[1] // ranks
    copies = []
    for k in range(ranks):
        at = pl.ds(pl.multiple_of((rank_ref[0] ^ k) * columns + start, HEAD_DIM), wide)
        copies.append(pltpu.make_async_copy(upstream_ref.at[:, at], out_ref.at[k], arrived.at[k]))
    for copy in copies:
        copy.start()
    for copy in copies:
        copy.wait()


def lead(rank, upstream, share, ranks):
    whole = pl.BlockSpec(memory_space=pl.ANY)
    return pl.pallas_call(
        functools.partial(lead_kernel, share, ranks),
        grid_spec=pltpu.PrefetchScalarGridSpec(
            num_scalar_prefetch=1,
            grid=(1,),
            in_specs=[whole],
            out_specs=whole,
            scratch_shapes=[pltpu.SemaphoreType.DMA((ranks,))],
        ),
        out_shape=made((ranks, upstream.shape[0], share[1])),
        compiler_params=params(4),
        cost_estimate=cost(0, upstream.size),
    )(rank, pinned(upstream))


def prepare_kernel(shares, ranks, steps, rank_ref, upstream_ref, inputs_ref, *refs):
    *out_refs, upstream_held, inputs_held, arrived = refs
    handed_refs, normed_refs = [None, *out_refs[: len(shares) - 1]], out_refs[len(shares) - 1 :]
    block_rows = inputs_ref.shape[0] // steps
    columns = inputs_ref.shape[1] // ranks
    step = pl.program_id(0)

    def copies(i):
        down = pl.ds(pl.multiple_of(i * block_rows, block_rows), block_rows)
        return [
            pltpu.make_async_copy(source.at[down, :], held.at[down, :], arrived.at[n, i])
            for n, (source, held) in enumerate(((inputs_ref, inputs_held), (upstream_ref, upstream_held)))
        ]

    @pl.when(step == 0)
    def _():
        for n in range(2):
            for i in range(steps):
                copies(i)[n].start()

    inputs_copy, upstream_copy = copies(step)
    inputs_copy.wait()
    down = pl.ds(pl.multiple_of(step * block_rows, block_rows), block_rows)
    x = inputs_held[down, :].astype(jnp.float32)
    inverse = 1.0 / jnp.sqrt(jnp.mean(x * x, axis=-1, keepdims=True) + EPSILON)
    for c, (start, wide) in enumerate(shares):
        for k in range(ranks):
            at = pl.ds(pl.multiple_of((rank_ref[0] ^ k) * columns + start, HEAD_DIM), wide)
            piece = inputs_held[down, at].astype(jnp.float32)
            normed_refs[c * ranks + k][...] = (piece * inverse).astype(jnp.bfloat16)
    upstream_copy.wait()
    for c, (start, wide) in list(enumerate(shares))[1:]:
        for k in range(ranks):
            at = pl.ds(pl.multiple_of((rank_ref[0] ^ k) * columns + start, HEAD_DIM), wide)
            handed_refs[c][k] = upstream_held[down, at]


def prepare(rank, upstream, inputs, shares, ranks, block_rows):
    length, features = inputs.shape
    steps = length // block_rows
    whole = pl.BlockSpec(memory_space=pl.ANY)

    def result(shape, near):
        return made(shape) if near else pltpu.HBM(shape, jnp.bfloat16)

    outs = pl.pallas_call(
        functools.partial(prepare_kernel, shares, ranks, steps),
        grid_spec=pltpu.PrefetchScalarGridSpec(
            num_scalar_prefetch=1,
            grid=(steps,),
            in_specs=[whole, whole],
            out_specs=[pl.BlockSpec((ranks, block_rows, wide), lambda i, _: (0, i, 0)) for _, wide in shares[1:]]
            + [pl.BlockSpec((block_rows, wide), lambda i, _: (i, 0)) for _, wide in shares for _ in range(ranks)],
            scratch_shapes=[pltpu.VMEM((length, features), jnp.bfloat16)] * 2
            + [pltpu.SemaphoreType.DMA((2, steps))],
        ),
        out_shape=[result((ranks, length, wide), False) for _, wide in shares[1:]]
        + [result((length, wide), c == 0 and k) for c, (_, wide) in enumerate(shares) for k in range(ranks)],
        compiler_params=params(14),
        cost_estimate=cost(4 * inputs.size, 8 * inputs.size),
    )(rank, pinned(upstream), pinned(inputs))
    normed = outs[len(shares) - 1 :]
    return outs[: len(shares) - 1], [normed[c * ranks : (c + 1) * ranks] for c in range(len(shares))]


def folded(x):
    return jnp.sum(x.reshape(x.shape[0] // 8, 8, x.shape[1]), axis=0)


def attention_kernel(ranks, rank_ref, *refs):
    normed_refs, grad_out_refs = refs[:ranks], refs[ranks : 2 * ranks]
    keys_ref, values_ref, gain_ref = refs[2 * ranks : 2 * ranks + 3]
    *grad_queries_refs, grad_keys_ref, grad_values_ref, grad_gain_ref = refs[-ranks - 10 : -7]
    normed_ref, out_ref, turned_ref, weights_ref, slopes_ref, value_sums, key_sums = refs[-7:]
    tokens = grad_queries_refs[0].shape[0]
    length, wide = keys_ref.shape
    block = min(BLOCK, length)
    blocks = length // block
    scaling = 1.0 / math.sqrt(HEAD_DIM)
    base = scaling * math.log2(math.e)

    def rows_of(k):
        return pl.ds(pl.multiple_of((rank_ref[0] ^ k) * tokens, tokens), tokens)

    for k in range(ranks):
        normed_ref[rows_of(k), :] = normed_refs[k][...]
        out_ref[rows_of(k), :] = grad_out_refs[k][0] if k == 0 else grad_out_refs[k][...]

    key_at = lax.broadcasted_iota(jnp.int32, (block, block), 0)
    query_at = lax.broadcasted_iota(jnp.int32, (block, block), 1)
    allowed = key_at <= query_at
    across = (((1,), (1,)), ((), ()))

    def rows(x, i):
        return x[i * block : (i + 1) * block]

    heads = []
    for n, start in enumerate(range(0, wide, HEAD_DIM)):
        at = slice(start, start + HEAD_DIM)
        keys = keys_ref[:, at]
        heads.append(
            dict(
                n=n,
                at=at,
                queries=(normed_ref[:, at].astype(jnp.float32) * gain_ref[:, at]).astype(jnp.bfloat16),
                grad_out=out_ref[:, at],
                keys=keys,
                values=values_ref[:, at],
                keys_turned=keys.T,
            )
        )

    def product(head, i, j):
        score = lax.dot_general(
            rows(head["keys"], j), rows(head["queries"], i), across, preferred_element_type=jnp.float32
        )
        weighed = lax.dot_general(
            rows(head["values"], j), rows(head["grad_out"], i), across, preferred_element_type=jnp.float32
        )
        score = jnp.where(allowed, score, -jnp.inf) if j == i else score
        return score, weighed, jnp.max(score.reshape(block // 8, 8, block), axis=0)

    def joined(x, y):
        return y if x is None else x + y

    def gradients(head, i):
        here, upto = slice(i * block, (i + 1) * block), slice(0, (i + 1) * block)
        held, at = head["n"], head["at"]
        weights, slopes = weights_ref[held, upto, here], slopes_ref[held, upto, here]
        turned = jnp.dot(head["keys_turned"][:, upto], slopes, preferred_element_type=jnp.float32)
        turned_ref[here, at] = turned.T.astype(jnp.bfloat16)
        for sums_ref, grad_ref, wide, x in (
            (value_sums, grad_values_ref, weights, head["grad_out"]),
            (key_sums, grad_keys_ref, slopes, head["queries"]),
        ):
            part = jnp.dot(wide, rows(x, i), preferred_element_type=jnp.float32)
            if i < blocks - 1:
                part = part + sums_ref[upto, at]
            grad_ref[here, at] = part[here].astype(jnp.bfloat16)
            if i:
                before = slice(0, i * block)
                sums_ref[before, at] = part[before]

    stages = [(head, i) for head in heads for i in reversed(range(blocks))]
    ready = [product(*stages[0], j) for j in range(stages[0][1] + 1)]
    for at, (head, i) in enumerate(stages):
        tiles, ready = ready, []
        later = [(*stages[at + 1], j) for j in range(stages[at + 1][1] + 1)] if at + 1 < len(stages) else []
        top = functools.reduce(jnp.maximum, [t[2] for t in tiles])
        shift = jnp.max(top, axis=0, keepdims=True) * base
        exps, total, slope = [], None, None
        for j, (score, weighed, _) in enumerate(tiles):
            e = jnp.exp2(score * base - shift)
            exps.append(e)
            total = joined(total, folded(e))
            slope = joined(slope, folded(e * weighed))
            if later:
                ready.append(product(*later.pop(0)))
        ready += [product(*one) for one in later]
        if at:
            gradients(*stages[at - 1])
        inverse = 1.0 / jnp.sum(total, axis=0, keepdims=True)
        delta = jnp.sum(slope, axis=0, keepdims=True) * inverse
        for j, (_, weighed, _) in enumerate(tiles):
            weights = exps[j] * inverse
            spot = (head["n"], slice(j * block, (j + 1) * block), slice(i * block, (i + 1) * block))
            weights_ref[spot] = weights.astype(jnp.bfloat16)
            slopes_ref[spot] = (weights * (weighed - delta) * scaling).astype(jnp.bfloat16)
    gradients(*stages[-1])

    grad_gain_ref[...] = jnp.sum(
        folded(turned_ref[...].astype(jnp.float32) * normed_ref[...].astype(jnp.float32)), axis=0, keepdims=True
    )
    for k, grad_queries_ref in enumerate(grad_queries_refs):
        grad_queries_ref[...] = turned_ref[rows_of(k), :]


def attention_back(share, rank, normed, grad_out, keys, values, gain, earlier):
    start, wide = share
    heads = wide // HEAD_DIM
    step = math.gcd(math.gcd(start, wide), HEADS_A_STEP * HEAD_DIM)
    first = start // step
    ranks, tokens = len(normed), normed[0].shape[0]
    length = keys.shape[0]
    own = pl.BlockSpec((tokens, step), lambda h, _: (0, h))
    first_piece = pl.BlockSpec((1, tokens, step), lambda h, _: (0, 0, h))
    placed = pl.BlockSpec((length, step), lambda h, _: (0, first + h))
    pairs = length * length * heads
    outs = pl.pallas_call(
        functools.partial(attention_kernel, ranks),
        grid_spec=pltpu.PrefetchScalarGridSpec(
            num_scalar_prefetch=1,
            grid=(wide // step,),
            in_specs=[own] * ranks
            + [first_piece]
            + [own] * (ranks - 1)
            + [placed, placed, pl.BlockSpec((1, step), lambda h, _: (0, first + h))]
            + [pl.BlockSpec(memory_space=pl.ANY)] * len(earlier),
            out_specs=[own] * ranks
            + [placed, placed, pl.BlockSpec((1, step), lambda h, _: (0, h))],
            scratch_shapes=[pltpu.VMEM((length, step), jnp.bfloat16)] * 3
            + [pltpu.VMEM((step // HEAD_DIM, length, length), jnp.bfloat16)] * 2
            + [pltpu.VMEM((length, step), jnp.float32)] * 2,
        ),
        out_shape=[made((tokens, wide))] * ranks
        + [pltpu.HBM(keys.shape, jnp.bfloat16)] * 2
        + [made((1, wide), jnp.float32)],
        input_output_aliases={2 * ranks + 4 + i: ranks + i for i in range(len(earlier))},
        compiler_params=params(20),
        cost_estimate=cost(10 * pairs * HEAD_DIM, 8 * pairs, pairs),
    )(rank, *normed, *grad_out, pinned(keys), pinned(values), gain, *earlier)
    return outs[:ranks], outs[ranks : ranks + 2], outs[-1]


def lanes(x):
    return sum(x[:, i : i + HEAD_DIM] for i in range(0, x.shape[1], HEAD_DIM))


def wide_piece(share, ranks, rank_ref, k, inputs_ref, gain_ref, grad_ref):
    start, wide = share
    columns = inputs_ref.shape[1] // ranks
    at = pl.ds(pl.multiple_of((rank_ref[0] ^ k) * columns + start, HEAD_DIM), wide)
    x = inputs_ref[:, at].astype(jnp.float32)
    return at, x, grad_ref[...].astype(jnp.float32) * gain_ref[:, at]


def begin_kernel(shares, ranks, rank_ref, inputs_ref, gain_ref, *refs):
    given, (inverse_ref, products_ref), base_refs = refs[: -len(shares) - 2], refs[-len(shares) - 2 : -len(shares)], refs[-len(shares) :]
    incoming_refs, grad_refs = given[: len(shares)], given[len(shares) :][::-1]
    x = inputs_ref[...].astype(jnp.float32)
    squares = lanes(x * x)
    mean = jnp.sum(squares, axis=-1, keepdims=True) / inputs_ref.shape[1]
    inverse = 1.0 / jnp.sqrt(mean + EPSILON)
    products = jnp.zeros(products_ref.shape, jnp.float32)
    for c, share in enumerate(shares):
        for k in range(ranks):
            _, x, scaled = wide_piece(share, ranks, rank_ref, k, inputs_ref, gain_ref, grad_refs[c * ranks + k])
            products += lanes(scaled * (x * inverse))
            base_refs[c][k] = incoming_refs[c][k].astype(jnp.float32) + scaled * inverse
    inverse_ref[...] = jnp.broadcast_to(inverse, inverse_ref.shape)
    products_ref[...] = products


def finish_kernel(shares, ranks, rank_ref, inputs_ref, gain_ref, inverse_ref, products_ref, *refs):
    *base_refs, incoming_ref = refs[: len(shares)]
    grad_refs, out_ref = refs[len(shares) : -1][::-1], refs[-1]
    features = inputs_ref.shape[1]
    inverse = inverse_ref[:, :1]
    products, last = products_ref[...], []
    for k in range(ranks):
        last.append(wide_piece(shares[-1], ranks, rank_ref, k, inputs_ref, gain_ref, grad_refs[k]))
        products += lanes(last[k][2] * (last[k][1] * inverse))
    slope = jnp.sum(products, axis=-1, keepdims=True) / features * inverse * inverse
    for (start, wide), base_ref in zip(shares, base_refs):
        for k in range(ranks):
            at = pl.ds(pl.multiple_of((rank_ref[0] ^ k) * (features // ranks) + start, HEAD_DIM), wide)
            out_ref[:, at] = (base_ref[k] - inputs_ref[:, at].astype(jnp.float32) * slope).astype(jnp.bfloat16)
    for k, (at, x, scaled) in enumerate(last):
        incoming = incoming_ref[k].astype(jnp.float32)
        out_ref[:, at] = (incoming + (scaled * inverse - x * slope)).astype(jnp.bfloat16)


def finish(rank, inputs, gain, incoming, grads, shares, block_rows):
    length, features = inputs.shape
    ranks = len(grads[0])
    flat = pl.BlockSpec((block_rows, features), lambda i, _: (i, 0))
    row = pl.BlockSpec((1, features), lambda i, _: (0, 0))
    narrow = pl.BlockSpec((block_rows, HEAD_DIM), lambda i, _: (i, 0))
    stacks = [pl.BlockSpec((ranks, block_rows, wide), lambda i, _: (0, i, 0)) for _, wide in shares]
    pieces = [[pl.BlockSpec((block_rows, wide), lambda i, _: (i, 0))] * ranks for _, wide in shares]
    before = len(shares) - 1

    def call(kernel, in_specs, out_specs, out_shape, share):
        return pl.pallas_call(
            functools.partial(kernel, shares[:before] if kernel is begin_kernel else shares, ranks),
            grid_spec=pltpu.PrefetchScalarGridSpec(
                num_scalar_prefetch=1, grid=(length // block_rows,), in_specs=in_specs, out_specs=out_specs
            ),
            out_shape=out_shape,
            compiler_params=params(20),
            cost_estimate=cost(12 * inputs.size, share * inputs.size),
        )

    inverse, products, *base = call(
        begin_kernel,
        [flat, row] + stacks[:before] + sum(pieces[:before], [])[::-1],
        [narrow, narrow] + stacks[:before],
        [made((length, HEAD_DIM), jnp.float32)] * 2
        + [made((ranks, length, wide), jnp.float32) for _, wide in shares[:before]],
        10,
    )(rank, inputs, gain, *incoming[:before], *sum(grads[:before], [])[::-1])
    result = call(
        finish_kernel,
        [flat, row, narrow, narrow] + stacks + pieces[before],
        flat,
        made(inputs.shape),
        6,
    )(rank, inputs, gain, inverse, products, *base, incoming[before], *grads[before][::-1])
    return result, inverse


def from_behind(x, axis, by):
    devices = lax.axis_size(axis)
    return lax.ppermute(x, axis, [(i, (i + by) % devices) for i in range(devices)])


def total(x, axis, events):
    passing, result = x, x
    for _ in range(lax.axis_size(axis) - 1):
        passing = from_behind(passing, axis, 1)
        result = result + after([passing], events)[0]
    return result


def after(values, events):
    return lax.optimization_barrier((tuple(values), tuple(events)))[0]


def swap(x, k):
    return lax.ppermute(x, "tensor", [(i, i ^ k) for i in range(lax.axis_size("tensor"))])


def swapped(pieces, earlier=None):
    results = [pieces[0]]
    for k, piece in enumerate(pieces[1:], 1):
        if earlier and piece is not None:
            (piece,) = after([piece], earlier[k : k + 1])
        results.append(piece if piece is None else swap(piece, k))
    return results


def body(upstream, inputs, keys, values, gain):
    ranks = lax.axis_size("tensor")
    tokens = inputs.shape[2]
    columns = keys.shape[3]
    shares = cut(columns)

    upstream, inputs = upstream[0, 0], inputs[0, 0]
    keys, values = keys[0, 0], values[0, 0]
    rank = lax.axis_index("tensor")
    gain_columns = lax.dynamic_slice_in_dim(gain, rank * columns, columns, 1)
    rank = rank[None]

    first = lead(rank, upstream, shares[0], ranks)
    (later,) = after([rank], [first])
    handed, normed = prepare(later, upstream, inputs, shares, ranks, min(64, tokens))
    latest = None
    for c, pieces in enumerate(normed):
        normed[c] = latest = swapped(pieces, latest)
    incoming = []
    for c, held in enumerate([first, *handed]):
        if c >= 2:
            (held,) = after([held], [incoming[c - 2]])
        incoming.append(from_behind(held, "pipe", -1))
    grad_out = []
    for held in incoming:
        latest = swapped([held] + [held[k] for k in range(1, ranks)], latest)
        grad_out.append(latest)

    grads, gain_parts, earlier = [], [], ()
    for c, share in enumerate(shares):
        if 0 < c < len(shares) - 1:
            grad_out[c] = list(after(grad_out[c], [incoming[c + 1]]))
        grad_queries, earlier, gain_part = attention_back(
            share, rank, normed[c], grad_out[c], keys, values, gain_columns, earlier
        )
        gain_parts.append(gain_part)
        ahead = grads[-1] if grads else None
        grads.append(swapped(grad_queries, ahead))
    grad_keys, grad_values = earlier
    (inputs,) = after([inputs], gain_parts[-1:])
    grad_inputs, begun = finish(rank, inputs, gain, incoming, grads, shares, min(128, tokens))
    grad_gain = total(jnp.concatenate(gain_parts, axis=1), "dp", [begun])
    return (
        grad_inputs[None, None],
        grad_keys[None, None],
        grad_values[None, None],
        grad_gain,
    )


def solution(mesh):
    in_specs = (
        P("pipe", "dp", "tensor", None),
        P("pipe", "dp", "tensor", None),
        P("pipe", "dp", None, "tensor"),
        P("pipe", "dp", None, "tensor"),
        P("pipe", None),
    )
    out_specs = (
        P("pipe", "dp", "tensor", None),
        P("pipe", "dp", None, "tensor"),
        P("pipe", "dp", None, "tensor"),
        P("pipe", "tensor"),
    )
    return jax.shard_map(body, mesh=mesh, in_specs=in_specs, out_specs=out_specs, check_vma=False)
```
